32 devices in a mesh: grp: 16 (over z, x, core), span: 2 (over y).
Axes of the slice: x: 2, y: 2, z: 4, core: 2. Of those that a mesh axis runs over, the one named last changes fastest.
Arguments:
- queries: bfloat16 [4096, 2240], P(('grp', 'span')), may hold values from -6 to 6
- key_rows: bfloat16 [4096, 2240], P(('grp', 'span')), may hold values from -6 to 6
- value_rows: bfloat16 [4096, 2240], P(('grp', 'span')), may hold values from -6 to 6
- retention: float32 [32, 20], P(('grp', 'span')), may hold values from 0.2 to 1, as said below
- up_weight: bfloat16 [2240, 2, 3072], P('grp', None, 'span'), may hold values from -0.125 to 0.125
- conv_weight: bfloat16 [3, 3, 3, 2, 3072], P(None, None, None, None, 'span'), may hold values from -1.25 to 1.25
- conv_bias: float32 [2, 3072], P(None, 'span'), may hold values from -3 to 3
Outputs:
- hidden: bfloat16 [4096, 3072], P('grp', 'span')
The draws below stay inside these ranges and needn't reach their ends.
Inputs may be any that keep to these rules, and one draw needn't show every extreme that they name: `retention`: retention factors of a head's carried state, one per time span.
All inputs are finite; a program needn't handle non-finite values.
Results may differ from the reference program's by a relative error of at most 0.015.
Values may be sent and summed in bfloat16 or wider, within the bound.
A program may use at most 128 MiB of HBM per device.

```python
import jax
import jax.numpy as jnp
from jax import lax

D = 2240
ATTENTION_LANES = 20
HD = 112
FFW = 3072
FH = 8
FW = 16
TOK_DEV = 128
CLIP_PORTIONS = 32
TOKENS = 4096
N_SPAN = 2


def draw_retention(key, part):
    lookup_embeddings = jax.random.split(key, 6)
    fast_share = 0.5
    fast_heads = jax.random.bernoulli(lookup_embeddings[0], fast_share, (1, ATTENTION_LANES))
    slow_rate = jax.random.uniform(lookup_embeddings[1], (1, ATTENTION_LANES), jnp.float32, 0.2, 0.6) / CLIP_PORTIONS
    jitter = jnp.exp(jax.random.uniform(lookup_embeddings[2], (CLIP_PORTIONS, ATTENTION_LANES), jnp.float32, -0.69, 0.69))
    gradual_fading_retain = jnp.exp(-slow_rate * jitter)
    fast_keep = jax.random.uniform(lookup_embeddings[3], (CLIP_PORTIONS, ATTENTION_LANES), jnp.float32, 0.2, 0.6)
    picture_groups = jax.random.bernoulli(lookup_embeddings[4], 3.0 / CLIP_PORTIONS, (CLIP_PORTIONS, 1))
    group_edge_position = jax.random.uniform(lookup_embeddings[5], (CLIP_PORTIONS, ATTENTION_LANES), jnp.float32, 0.5, 0.8)
    gradual_fading_retain = jnp.where(picture_groups, gradual_fading_retain * group_edge_position, gradual_fading_retain)
    return jnp.where(fast_heads, fast_keep, gradual_fading_retain).astype(jnp.float32)


def block_scale(rng, shape, cuts, smallest, largest):
    def one(position, shards_of):
        steps = jax.random.uniform(jax.random.fold_in(jax.random.fold_in(rng, 6), position), (shards_of,), jnp.float32, smallest / len(cuts), largest / len(cuts))
        return jnp.repeat(jnp.exp(steps), shape[position] // shards_of).reshape((-1,) + (1,) * (len(shape) - position - 1))

    gain = one(*cuts[0])
    for cut in cuts[1:]:
        gain = gain * one(*cut)
    return gain


def noise(own_key, extent, scale, limit, cuts=(), kind=jnp.bfloat16):
    array = jax.random.normal(own_key, extent, jnp.float32) * scale
    if len(cuts) > 0:
        array = block_scale(own_key, extent, cuts, -0.22, 0.18) * array
    return jnp.clip(array, min=-limit, max=limit).astype(kind)


def setup_inputs(seed: int = 0) -> dict:
    splits = jax.random.split(jax.random.key(seed), 8)
    queries = noise(splits[0], (TOKENS, D), 1.0, 6.0, ((0, 32),))
    key_rows = noise(splits[1], (TOKENS, D), 1.0, 6.0, ((0, 32),))
    value_rows = noise(splits[2], (TOKENS, D), 1.0, 6.0, ((0, 32),))
    retention = draw_retention(jax.random.fold_in(splits[7], 71), 0)
    up_weight = noise(splits[4], (D, 2, FFW), D ** -0.5, 0.125, ((0, 16), (2, 2)))
    conv_weight = noise(splits[5], (3, 3, 3, 2, FFW), 27 ** -0.5, 1.25, ((4, 2),))
    conv_bias = noise(splits[6], (2, FFW), 0.5, 3.0, ((1, 2),), jnp.float32)
    return dict(queries=queries, key_rows=key_rows, value_rows=value_rows, retention=retention, up_weight=up_weight, conv_weight=conv_weight, conv_bias=conv_bias)


def attention(queries, key_rows, value_rows, retention):
    shape = (CLIP_PORTIONS, TOK_DEV, ATTENTION_LANES, HD)
    q_blocks = jnp.maximum(queries, 0).reshape(shape)
    k_blocks = jnp.maximum(key_rows, 0).reshape(shape)
    v_blocks = value_rows.reshape(shape)

    def advance(carry, inputs):
        state_prev, sum_prev = carry
        q_span, k_span, v_span, factor = inputs
        q_float = q_span.astype(jnp.float32)
        k_float = k_span.astype(jnp.float32)
        local_state = jnp.einsum('thd,the->hde', k_float, v_span.astype(jnp.float32), precision=lax.Precision.HIGHEST)
        local_sum = lax.optimization_barrier(jnp.sum(k_float, axis=0))
        state = factor[:, None, None] * state_prev + local_state
        key_sum = factor[:, None] * sum_prev + local_sum
        numer = jnp.einsum('thd,hde->the', q_float, state, precision=lax.Precision.HIGHEST)
        denom = jnp.einsum('thd,hd->th', q_float, key_sum, precision=lax.Precision.HIGHEST) + 0.0001
        return ((state, key_sum), numer / denom[:, :, None])
    start = (jnp.zeros((ATTENTION_LANES, HD, HD), jnp.float32), jnp.zeros((ATTENTION_LANES, HD), jnp.float32))
    final, outputs = lax.scan(advance, start, (q_blocks, k_blocks, v_blocks, retention))
    return outputs.reshape(TOKENS, D)

def reference(queries, key_rows, value_rows, retention, up_weight, conv_weight, conv_bias):
    attended = attention(queries, key_rows, value_rows, retention)
    scale = lax.rsqrt(lax.optimization_barrier(jnp.mean(attended * attended, axis=-1, keepdims=True)) + 1e-06)
    normed = (attended * scale).astype(jnp.bfloat16)
    blocks = N_SPAN
    width = FFW // blocks
    w_blocks = up_weight.reshape(D, 2, blocks, width).transpose(2, 0, 1, 3)
    k_blocks = conv_weight.reshape(3, 3, 3, 2, blocks, width).transpose(4, 0, 1, 2, 3, 5)
    b_blocks = conv_bias.reshape(2, blocks, width).transpose(1, 0, 2)

    def one_block(inputs):
        w_block, k_block, bias_block_rows = inputs
        up_vals = jnp.dot(normed, w_block.reshape(D, 2 * width), preferred_element_type=jnp.float32).astype(jnp.bfloat16)
        grid = up_vals.reshape(CLIP_PORTIONS, FH, FW, 2 * width)
        padded = jnp.pad(grid, ((1, 1), (1, 1), (1, 1), (0, 0)))
        mixed = jnp.zeros((CLIP_PORTIONS, FH, FW, 2 * width), jnp.float32) + bias_block_rows.reshape(2 * width)
        for tap_t in range(3):
            for tap_y in range(3):
                for tap_x in range(3):
                    visible_extent = padded[tap_t:tap_t + CLIP_PORTIONS, tap_y:tap_y + FH, tap_x:tap_x + FW]
                    mixed = mixed + visible_extent.astype(jnp.float32) * k_block[tap_t, tap_y, tap_x].reshape(2 * width).astype(jnp.float32)
        mixed = mixed.reshape(TOKENS, 2, width)
        return (mixed[:, 0] * jax.nn.silu(mixed[:, 1])).astype(jnp.bfloat16)
    results = lax.map(one_block, (w_blocks, k_blocks, b_blocks))
    return results.transpose(1, 0, 2).reshape(TOKENS, FFW)
```

```python
import functools

import jax
import jax.numpy as jnp
from jax import lax
from jax.experimental import pallas as pl
from jax.experimental.pallas import tpu as pltpu
from jax.sharding import PartitionSpec as P

FH = 8
FW = 16
BLOCK = 8
MESH = pl.DeviceIdType.MESH


def swap(x, groups):
    return lax.ppermute(x, "grp", [(i, i ^ 1) for i in range(groups)])


def fused(groups, members, heads, head_dim, kt_ref, v_ref, q_ref, ret_ref, w_ref, wg_ref, nrm_ref,
          local, outbox, inbox, tot_out, tot_in, back_out, back_in, within, attend, normed,
          s1, r1, s2, r2, s3, r3, sw, rw, sx, rx, sn, rn, sc, rc, lsem):
    grp = lax.axis_index("grp")
    span = lax.axis_index("span")
    me = grp * members + span
    spot = me % BLOCK
    layer = me // BLOCK
    layers = groups * members // BLOCK
    core = grp % 2
    chip = grp // 2
    chips = groups // 2
    rows = heads * head_dim // BLOCK

    def device(r):
        return (r // members, r % members)

    even = chip % 2 == 0
    place = jnp.where(even, chip // 2, chips - 1 - chip // 2)

    def chip_at(p):
        p = (p + chips) % chips
        return jnp.where(p < chips // 2, 2 * p, 2 * (chips - 1 - p) + 1)

    right = (2 * chip_at(place + 1) + core, span)
    left = (2 * chip_at(place - 1) + core, span)
    twin = (2 * chip + 1 - core, span)
    mates = [(spot + k) % BLOCK for k in range(1, BLOCK)]
    others = [(layer + k) % layers for k in range(1, layers)]

    barrier = pltpu.get_barrier_semaphore()
    targets = [device(layer * BLOCK + m) for m in mates]
    targets += [device(o * BLOCK + spot) for o in others]
    targets += [right, left, twin]
    for t in targets:
        pl.semaphore_signal(barrier, inc=1, device_id=t, device_id_type=MESH)
    pl.semaphore_wait(barrier, len(targets))

    def send(src, dst, ssem, rsem, to):
        return pltpu.make_async_remote_copy(
            src_ref=src, dst_ref=dst, send_sem=ssem, recv_sem=rsem, device_id=to, device_id_type=MESH
        )

    across = send(w_ref.at[1 - core], wg_ref.at[chip, core], sx, rx, twin)
    across.start()
    keep = pltpu.make_async_copy(w_ref.at[core], wg_ref.at[chip, core], lsem.at[0])
    keep.start()

    half = chips // 2

    def halves(way, hop):
        if hop == half - 1:
            return (way,)
        return (0, 1)

    def hop_copy(way, hop, part):
        source = chip_at(place - hop) if way == 0 else chip_at(place + hop)
        at = wg_ref.at[source, part]
        return send(at, at, sw.at[way, hop, part], rw.at[way, hop, part], right if way == 0 else left)

    def hop_wait(way, hop, part):
        source = chip_at(place - hop - 1) if way == 0 else chip_at(place + hop + 1)
        at = wg_ref.at[source, part]
        send(at, at, sw.at[way, hop, part], rw.at[way, hop, part], right if way == 0 else left).wait_recv()

    started = []

    def ring(hop):
        for way in (0, 1):
            if hop == 0:
                continue
            for part in halves(way, hop - 1):
                hop_wait(way, hop - 1, part)
        if hop < half:
            for way in (0, 1):
                for part in halves(way, hop):
                    c = hop_copy(way, hop, part)
                    c.start()
                    started.append(c)

    lane = lax.broadcasted_iota(jnp.int32, (head_dim, 128), 1)
    for h in range(heads):
        state = jnp.dot(kt_ref[h], v_ref[h], preferred_element_type=jnp.float32)
        keepf = jnp.full((head_dim, 128), ret_ref[0, h], jnp.float32)
        high = keepf.astype(jnp.bfloat16).astype(jnp.float32)
        state = jnp.where(lane == head_dim + 1, high, state)
        state = jnp.where(lane == head_dim + 2, keepf - high, state)
        local[h * head_dim : (h + 1) * head_dim, :] = state
    for j in range(BLOCK):
        outbox[j] = local[j * rows : (j + 1) * rows, :].astype(jnp.bfloat16)
    pltpu.make_async_copy(outbox.at[spot], inbox.at[spot], lsem.at[1]).start()
    first = [
        send(outbox.at[m], inbox.at[spot], s1.at[m], r1.at[spot], device(layer * BLOCK + m)) for m in mates
    ]
    for c in first:
        c.start()

    keep.wait()
    across.wait()
    ring(0)

    pltpu.make_async_copy(outbox.at[spot], inbox.at[spot], lsem.at[1]).wait()
    for m in mates:
        send(outbox.at[m], inbox.at[m], s1.at[m], r1.at[m], device(layer * BLOCK + m)).wait_recv()
    wide = lax.broadcasted_iota(jnp.int32, (rows, 128), 1)

    def factor_of(x):
        return x[:, head_dim + 1 : head_dim + 2] + x[:, head_dim + 2 : head_dim + 3]

    running = jnp.zeros((rows, 128), jnp.float32)
    factor = jnp.ones((rows, 1), jnp.float32)
    factors = []
    for j in range(BLOCK):
        within[j] = running
        factors.append(factor)
        got = inbox[j].astype(jnp.float32)
        f = factor_of(got)
        running = f * running + got
        factor = factor * f
    full = jnp.broadcast_to(factor, (rows, 128))
    high = full.astype(jnp.bfloat16).astype(jnp.float32)
    total = jnp.where(wide == head_dim + 1, high, running)
    total = jnp.where(wide == head_dim + 2, full - high, total)
    tot_out[...] = total.astype(jnp.bfloat16)
    second = [
        send(tot_out, tot_in.at[layer], s2.at[o], r2.at[layer], device(o * BLOCK + spot)) for o in others
    ]
    for c in second:
        c.start()
    for o in others:
        send(tot_out, tot_in.at[o], s2.at[o], r2.at[o], device(o * BLOCK + spot)).wait_recv()

    def earlier(i, carry):
        got = tot_in[i].astype(jnp.float32)
        return factor_of(got) * carry + got

    before = lax.fori_loop(0, layer, earlier, jnp.zeros((rows, 128), jnp.float32))
    for j in range(BLOCK):
        back_out[j] = (factors[j] * before + within[j]).astype(jnp.bfloat16)
    pltpu.make_async_copy(back_out.at[spot], back_in.at[spot], lsem.at[2]).start()
    third = [
        send(back_out.at[m], back_in.at[spot], s3.at[m], r3.at[spot], device(layer * BLOCK + m)) for m in mates
    ]
    for c in third:
        c.start()
    pltpu.make_async_copy(back_out.at[spot], back_in.at[spot], lsem.at[2]).wait()
    for m in mates:
        send(back_out.at[m], back_in.at[m], s3.at[m], r3.at[m], device(layer * BLOCK + m)).wait_recv()
    for j in range(BLOCK):
        part = slice(j * rows, (j + 1) * rows)
        got = local[part, :]
        local[part, :] = factor_of(got) * back_in[j].astype(jnp.float32) + got

    squares = jnp.zeros((128, 1), jnp.float32)
    column = lax.broadcasted_iota(jnp.int32, (q_ref.shape[1], 128), 1)
    for h in range(heads):
        state = local[h * head_dim : (h + 1) * head_dim, :].astype(jnp.bfloat16)
        numer = jnp.dot(q_ref[h], state, preferred_element_type=jnp.float32)
        value = numer / (numer[:, head_dim : head_dim + 1] + 0.0001)
        value = jnp.where(column < head_dim, value, 0.0)
        squares = squares + jnp.sum(value * value, axis=1, keepdims=True)
        attend[h] = value
    scale = lax.rsqrt(squares / (heads * head_dim) + 1e-06)
    for h in range(heads):
        normed[h] = (attend[h] * scale).astype(jnp.bfloat16)
    keepn = pltpu.make_async_copy(normed, nrm_ref.at[core, span], lsem.at[3])
    keepn.start()
    peers = [(span + k) % members for k in range(1, members)]
    fourth = [
        send(normed, nrm_ref.at[core, span], sn.at[p], rn.at[span], (grp, p)) for p in peers
    ]
    for c in fourth:
        c.start()
    cross = [send(normed, nrm_ref.at[core, span], sc.at[span], rc.at[span], twin)]
    cross[0].start()
    ring(1)
    for p in peers:
        send(normed, nrm_ref.at[core, p], sn.at[p], rn.at[p], (grp, p)).wait_recv()
        c = send(nrm_ref.at[core, p], nrm_ref.at[core, p], sc.at[p], rc.at[p], twin)
        c.start()
        cross.append(c)
    for hop in range(2, half + 1):
        ring(hop)
    keepn.wait()
    for p in [span] + peers:
        send(nrm_ref.at[1 - core, p], nrm_ref.at[1 - core, p], sc.at[p], rc.at[p], twin).wait_recv()
    for c in first + second + third + fourth + cross + started:
        c.wait_send()


def gather_and_attend(queries, key_rows, value_rows, retention, up_weight):
    groups = lax.axis_size("grp")
    members = lax.axis_size("span")
    tokens, dim = queries.shape
    heads = retention.shape[1]
    head_dim = dim // heads
    rows, _, width = up_weight.shape
    part = width // 2
    depth = -(-rows // 16) * 16
    kt = jnp.maximum(key_rows, 0).T.reshape(heads, head_dim, tokens)
    q = jnp.maximum(queries, 0).reshape(tokens, heads, head_dim).transpose(1, 0, 2)
    v = value_rows.reshape(tokens, heads, head_dim).transpose(1, 0, 2)
    rest = 128 - head_dim
    one = jnp.ones((heads, tokens, 1), v.dtype)
    v = jnp.concatenate([v, one, jnp.zeros((heads, tokens, rest - 1), v.dtype)], axis=2)
    w = up_weight.reshape(rows, 2, 2, part).transpose(2, 0, 1, 3).reshape(2, rows, width)
    w = jnp.pad(w, ((0, 0), (0, depth - rows), (0, 0)))
    chips = groups // 2
    share = dim // BLOCK
    layers = groups * members // BLOCK
    dma = pltpu.SemaphoreType.DMA
    vmem = pl.BlockSpec(memory_space=pltpu.VMEM)
    anywhere = pl.BlockSpec(memory_space=pl.ANY)
    bf = jnp.bfloat16
    slabs = pltpu.VMEM((BLOCK, share, 128), bf)
    weight, normed = pl.pallas_call(
        functools.partial(fused, groups, members, heads, head_dim),
        out_shape=(
            jax.ShapeDtypeStruct((chips, 2, depth, width), bf),
            jax.ShapeDtypeStruct((2, members, heads, tokens, 128), bf),
        ),
        in_specs=[vmem, vmem, vmem, pl.BlockSpec(memory_space=pltpu.SMEM), anywhere],
        out_specs=(anywhere, anywhere),
        scratch_shapes=[
            pltpu.VMEM((dim, 128), jnp.float32),
            slabs,
            slabs,
            pltpu.VMEM((share, 128), bf),
            pltpu.VMEM((layers, share, 128), bf),
            slabs,
            slabs,
            pltpu.VMEM((BLOCK, share, 128), jnp.float32),
            pltpu.VMEM((heads, tokens, 128), jnp.float32),
            pltpu.VMEM((heads, tokens, 128), bf),
            dma((BLOCK,)), dma((BLOCK,)),
            dma((layers,)), dma((layers,)),
            dma((BLOCK,)), dma((BLOCK,)),
            dma((2, chips // 2, 2)), dma((2, chips // 2, 2)),
            dma, dma,
            dma((members,)), dma((members,)),
            dma((members,)), dma((members,)),
            dma((4,)),
        ],
        compiler_params=pltpu.CompilerParams(
            collective_id=0, has_side_effects=True, vmem_limit_bytes=32 * 1024 * 1024
        ),
        name="gather_and_attend",
    )(kt, v, q, retention, w)
    weight = weight.reshape(groups * depth, width)
    normed = normed.reshape(2 * members, heads, tokens, 128)[..., :head_dim]
    normed = normed.transpose(0, 2, 1, 3).reshape(2 * members * tokens, groups, rows)
    normed = jnp.pad(normed, ((0, 0), (0, 0), (0, depth - rows)))
    return normed.reshape(2 * members * tokens, groups * depth), weight


def shards(queries, key_rows, value_rows, retention, up_weight, conv_weight, conv_bias):
    normed, flat_weight = gather_and_attend(queries, key_rows, value_rows, retention, up_weight)
    groups = lax.axis_size("grp")
    core = lax.axis_index("grp") % 2
    up_vals = jnp.dot(normed, flat_weight, preferred_element_type=jnp.float32)
    up_vals = up_vals.astype(jnp.bfloat16)
    part = flat_weight.shape[1] // 2
    frames = up_vals.shape[0] // (FH * FW)
    grid = up_vals.reshape(frames, FH, FW, 2 * part)
    onward = [(i, i + 2) for i in range(groups - 2)]
    before = lax.ppermute(grid[-1:], "grp", onward)
    after = lax.ppermute(grid[:1], "grp", [(j, i) for i, j in onward])
    extended = jnp.concatenate([before, grid, after], axis=0)
    padded = jnp.pad(extended, ((0, 0), (1, 1), (1, 1), (0, 0)))
    taps = lax.dynamic_slice_in_dim(conv_weight, core * part, part, axis=4)
    convolution_kernel = taps.reshape(3, 3, 3, 2 * part).astype(jnp.float32)
    bias = lax.dynamic_slice_in_dim(conv_bias, core * part, part, axis=1)
    mixed = jnp.zeros((frames, FH, FW, 2 * part), jnp.float32) + bias.reshape(2 * part)
    for tap_t in range(3):
        for tap_y in range(3):
            for tap_x in range(3):
                visible_extent = padded[
                    tap_t : tap_t + frames, tap_y : tap_y + FH, tap_x : tap_x + FW
                ]
                mixed = (
                    mixed
                    + visible_extent.astype(jnp.float32) * convolution_kernel[tap_t, tap_y, tap_x]
                )
    mixed = mixed.reshape(2, frames * FH * FW // 2, 2, part)
    hidden = (mixed[:, :, 0] * jax.nn.silu(mixed[:, :, 1])).astype(jnp.bfloat16)
    mine = lax.dynamic_index_in_dim(hidden, core, 0, False)
    theirs = swap(lax.dynamic_index_in_dim(hidden, 1 - core, 0, False), groups)
    first = jnp.where(core == 0, mine, theirs)
    second = jnp.where(core == 0, theirs, mine)
    return jnp.concatenate([first, second], axis=1)


def solution(mesh):
    in_specs = (
        P(("grp", "span"), None),
        P(("grp", "span"), None),
        P(("grp", "span"), None),
        P(("grp", "span"), None),
        P("grp", None, "span"),
        P(None, None, None, None, "span"),
        P(None, "span"),
    )
    out_specs = P("grp", "span")
    return jax.shard_map(shards, mesh=mesh, in_specs=in_specs, out_specs=out_specs, check_vma=False)
```

```python
import functools

import jax
import jax.numpy as jnp
from jax import lax
from jax.experimental import pallas as pl
from jax.experimental.pallas import tpu as pltpu
from jax.sharding import PartitionSpec as P

FH = 8
FW = 16
BLOCK = 8
MESH = pl.DeviceIdType.MESH


def swap(x, groups):
    return lax.ppermute(x, "grp", [(i, i ^ 1) for i in range(groups)])


def fused(groups, members, heads, head_dim, kt_ref, v_ref, q_ref, ret_ref, w_ref, wg_ref, nrm_ref,
          local, outbox, inbox, tot_out, tot_in, back_out, back_in, within, attend, normed,
          s1, r1, s2, r2, s3, r3, sw, rw, sx, rx, sn, rn, sc, rc, lsem):
    grp = lax.axis_index("grp")
    span = lax.axis_index("span")
    me = grp * members + span
    spot = me % BLOCK
    layer = me // BLOCK
    layers = groups * members // BLOCK
    core = grp % 2
    chip = grp // 2
    chips = groups // 2
    rows = heads * head_dim // BLOCK

    def device(r):
        return (r // members, r % members)

    even = chip % 2 == 0
    place = jnp.where(even, chip // 2, chips - 1 - chip // 2)

    def chip_at(p):
        p = (p + chips) % chips
        return jnp.where(p < chips // 2, 2 * p, 2 * (chips - 1 - p) + 1)

    right = (2 * chip_at(place + 1) + core, span)
    left = (2 * chip_at(place - 1) + core, span)
    twin = (2 * chip + 1 - core, span)
    mates = [(spot + k) % BLOCK for k in range(1, BLOCK)]
    others = [(layer + k) % layers for k in range(1, layers)]

    barrier = pltpu.get_barrier_semaphore()
    targets = [device(layer * BLOCK + m) for m in mates]
    targets += [device(o * BLOCK + spot) for o in others]
    targets += [right, left, twin]
    for t in targets:
        pl.semaphore_signal(barrier, inc=1, device_id=t, device_id_type=MESH)
    pl.semaphore_wait(barrier, len(targets))

    def send(src, dst, ssem, rsem, to):
        return pltpu.make_async_remote_copy(
            src_ref=src, dst_ref=dst, send_sem=ssem, recv_sem=rsem, device_id=to, device_id_type=MESH
        )

    across = send(w_ref.at[1 - core], wg_ref.at[chip, core], sx, rx, twin)
    across.start()
    keep = pltpu.make_async_copy(w_ref.at[core], wg_ref.at[chip, core], lsem.at[0])
    keep.start()

    half = chips // 2

    def halves(way, hop):
        if hop == half - 1:
            return (way,)
        return (0, 1)

    def hop_copy(way, hop, part):
        source = chip_at(place - hop) if way == 0 else chip_at(place + hop)
        at = wg_ref.at[source, part]
        return send(at, at, sw.at[way, hop, part], rw.at[way, hop, part], right if way == 0 else left)

    def hop_wait(way, hop, part):
        source = chip_at(place - hop - 1) if way == 0 else chip_at(place + hop + 1)
        at = wg_ref.at[source, part]
        send(at, at, sw.at[way, hop, part], rw.at[way, hop, part], right if way == 0 else left).wait_recv()

    started = []

    def launch(hop):
        for part in (0, 1):
            for way in (0, 1):
                if part in halves(way, hop):
                    c = hop_copy(way, hop, part)
                    c.start()
                    started.append(c)

    steps = [(hop, part) for hop in range(1, half + 1) for part in (0, 1)]

    def ring(count):
        for _ in range(min(count, len(steps))):
            hop, part = steps.pop(0)
            for way in (0, 1):
                if part in halves(way, hop - 1):
                    hop_wait(way, hop - 1, part)
                if hop < half and part in halves(way, hop):
                    c = hop_copy(way, hop, part)
                    c.start()
                    started.append(c)

    lane = lax.broadcasted_iota(jnp.int32, (head_dim, 128), 1)
    for h in range(heads):
        if h == 4:
            keep.wait()
            across.wait()
            launch(0)
        state = jnp.dot(kt_ref[h], v_ref[h], preferred_element_type=jnp.float32)
        keepf = jnp.full((head_dim, 128), ret_ref[0, h], jnp.float32)
        high = keepf.astype(jnp.bfloat16).astype(jnp.float32)
        state = jnp.where(lane == head_dim + 1, high, state)
        state = jnp.where(lane == head_dim + 2, keepf - high, state)
        local[h * head_dim : (h + 1) * head_dim, :] = state
    for j in range(BLOCK):
        outbox[j] = local[j * rows : (j + 1) * rows, :].astype(jnp.bfloat16)
    pltpu.make_async_copy(outbox.at[spot], inbox.at[spot], lsem.at[1]).start()
    first = [
        send(outbox.at[m], inbox.at[spot], s1.at[m], r1.at[spot], device(layer * BLOCK + m)) for m in mates
    ]
    for c in first:
        c.start()

    pltpu.make_async_copy(outbox.at[spot], inbox.at[spot], lsem.at[1]).wait()
    for m in mates:
        send(outbox.at[m], inbox.at[m], s1.at[m], r1.at[m], device(layer * BLOCK + m)).wait_recv()
    wide = lax.broadcasted_iota(jnp.int32, (rows, 128), 1)

    def factor_of(x):
        return x[:, head_dim + 1 : head_dim + 2] + x[:, head_dim + 2 : head_dim + 3]

    running = jnp.zeros((rows, 128), jnp.float32)
    factor = jnp.ones((rows, 1), jnp.float32)
    factors = []
    for j in range(BLOCK):
        within[j] = running
        factors.append(factor)
        got = inbox[j].astype(jnp.float32)
        f = factor_of(got)
        running = f * running + got
        factor = factor * f
    full = jnp.broadcast_to(factor, (rows, 128))
    high = full.astype(jnp.bfloat16).astype(jnp.float32)
    total = jnp.where(wide == head_dim + 1, high, running)
    total = jnp.where(wide == head_dim + 2, full - high, total)
    tot_out[...] = total.astype(jnp.bfloat16)
    second = [
        send(tot_out, tot_in.at[layer], s2.at[o], r2.at[layer], device(o * BLOCK + spot)) for o in others
    ]
    for c in second:
        c.start()
    ring(1)
    for o in others:
        send(tot_out, tot_in.at[o], s2.at[o], r2.at[o], device(o * BLOCK + spot)).wait_recv()

    def earlier(i, carry):
        got = tot_in[i].astype(jnp.float32)
        return factor_of(got) * carry + got

    before = lax.fori_loop(0, layer, earlier, jnp.zeros((rows, 128), jnp.float32))
    for j in range(BLOCK):
        back_out[j] = (factors[j] * before + within[j]).astype(jnp.bfloat16)
    pltpu.make_async_copy(back_out.at[spot], back_in.at[spot], lsem.at[2]).start()
    third = [
        send(back_out.at[m], back_in.at[spot], s3.at[m], r3.at[spot], device(layer * BLOCK + m)) for m in mates
    ]
    for c in third:
        c.start()
    ring(1)
    pltpu.make_async_copy(back_out.at[spot], back_in.at[spot], lsem.at[2]).wait()
    for m in mates:
        send(back_out.at[m], back_in.at[m], s3.at[m], r3.at[m], device(layer * BLOCK + m)).wait_recv()
    for j in range(BLOCK):
        part = slice(j * rows, (j + 1) * rows)
        got = local[part, :]
        local[part, :] = factor_of(got) * back_in[j].astype(jnp.float32) + got

    ring(1)
    cut = heads * head_dim // groups
    depth = w_ref.shape[1]
    attend[...] = jnp.zeros_like(attend)
    squares = jnp.zeros((q_ref.shape[1], 1), jnp.float32)
    column = lax.broadcasted_iota(jnp.int32, (q_ref.shape[1], 128), 1)
    for h in range(heads):
        state = local[h * head_dim : (h + 1) * head_dim, :].astype(jnp.bfloat16)
        numer = jnp.dot(q_ref[h], state, preferred_element_type=jnp.float32)
        value = numer / (numer[:, head_dim : head_dim + 1] + 0.0001)
        value = jnp.where(column < head_dim, value, 0.0)
        squares = squares + jnp.sum(value * value, axis=1, keepdims=True)
        at, stop = h * head_dim, (h + 1) * head_dim
        while at < stop:
            block = at // cut
            end = min(stop, (block + 1) * cut)
            to = block * depth + at - block * cut
            attend[:, to : to + end - at] = value[:, at - h * head_dim : end - h * head_dim]
            at = end
    ring(1)
    scale = lax.rsqrt(squares / (heads * head_dim) + 1e-06)
    normed[...] = (attend[...] * scale).astype(jnp.bfloat16)
    keepn = pltpu.make_async_copy(normed, nrm_ref.at[core, span], lsem.at[3])
    keepn.start()
    peers = [(span + k) % members for k in range(1, members)]
    fourth = [
        send(normed, nrm_ref.at[core, span], sn.at[p], rn.at[span], (grp, p)) for p in peers
    ]
    for c in fourth:
        c.start()
    cross = [send(normed, nrm_ref.at[core, span], sc.at[span], rc.at[span], twin)]
    cross[0].start()
    ring(2)
    for p in peers:
        send(normed, nrm_ref.at[core, p], sn.at[p], rn.at[p], (grp, p)).wait_recv()
        c = send(nrm_ref.at[core, p], nrm_ref.at[core, p], sc.at[p], rc.at[p], twin)
        c.start()
        cross.append(c)
    ring(len(steps))
    keepn.wait()
    for p in [span] + peers:
        send(nrm_ref.at[1 - core, p], nrm_ref.at[1 - core, p], sc.at[p], rc.at[p], twin).wait_recv()
    for c in first + second + third + fourth + cross + started:
        c.wait_send()


def gather_and_attend(queries, key_rows, value_rows, retention, up_weight):
    groups = lax.axis_size("grp")
    members = lax.axis_size("span")
    tokens, dim = queries.shape
    heads = retention.shape[1]
    head_dim = dim // heads
    rows, _, width = up_weight.shape
    part = width // 2
    depth = -(-rows // 16) * 16
    kt = jnp.maximum(key_rows, 0).T.reshape(heads, head_dim, tokens)
    q = jnp.maximum(queries, 0).reshape(tokens, heads, head_dim).transpose(1, 0, 2)
    v = value_rows.reshape(tokens, heads, head_dim).transpose(1, 0, 2)
    rest = 128 - head_dim
    one = jnp.ones((heads, tokens, 1), v.dtype)
    v = jnp.concatenate([v, one, jnp.zeros((heads, tokens, rest - 1), v.dtype)], axis=2)
    w = up_weight.reshape(rows, 2, 2, part).transpose(2, 0, 1, 3).reshape(2, rows, width)
    w = jnp.pad(w, ((0, 0), (0, depth - rows), (0, 0)))
    chips = groups // 2
    share = dim // BLOCK
    layers = groups * members // BLOCK
    dma = pltpu.SemaphoreType.DMA
    vmem = pl.BlockSpec(memory_space=pltpu.VMEM)
    anywhere = pl.BlockSpec(memory_space=pl.ANY)
    bf = jnp.bfloat16
    slabs = pltpu.VMEM((BLOCK, share, 128), bf)
    weight, normed = pl.pallas_call(
        functools.partial(fused, groups, members, heads, head_dim),
        out_shape=(
            jax.ShapeDtypeStruct((chips, 2, depth, width), bf),
            jax.ShapeDtypeStruct((2, members, tokens, groups * depth), bf),
        ),
        in_specs=[vmem, vmem, vmem, pl.BlockSpec(memory_space=pltpu.SMEM), anywhere],
        out_specs=(anywhere, anywhere),
        scratch_shapes=[
            pltpu.VMEM((dim, 128), jnp.float32),
            slabs,
            slabs,
            pltpu.VMEM((share, 128), bf),
            pltpu.VMEM((layers, share, 128), bf),
            slabs,
            slabs,
            pltpu.VMEM((BLOCK, share, 128), jnp.float32),
            pltpu.VMEM((tokens, groups * depth), jnp.float32),
            pltpu.VMEM((tokens, groups * depth), bf),
            dma((BLOCK,)), dma((BLOCK,)),
            dma((layers,)), dma((layers,)),
            dma((BLOCK,)), dma((BLOCK,)),
            dma((2, chips // 2, 2)), dma((2, chips // 2, 2)),
            dma, dma,
            dma((members,)), dma((members,)),
            dma((members,)), dma((members,)),
            dma((4,)),
        ],
        compiler_params=pltpu.CompilerParams(
            collective_id=0, has_side_effects=True, vmem_limit_bytes=32 * 1024 * 1024
        ),
        name="gather_and_attend",
    )(kt, v, q, retention, w)
    weight = weight.reshape(groups * depth, width)
    return normed.reshape(2 * members * tokens, groups * depth), weight


def convolve(xv, xg, bv, bg, av, ag, tv, tg, cv, cg, out, pv, pg):
    frames = xv.shape[0]
    for x, before, after, pad in ((xv, bv, av, pv), (xg, bg, ag, pg)):
        pad[:, 0:1] = jnp.zeros_like(pad[:, 0:1])
        pad[:, FH + 1 :] = jnp.zeros_like(pad[:, FH + 1 :])
        pad[0:1, 1 : FH + 1] = before[...].astype(jnp.float32)
        pad[frames + 1 :, 1 : FH + 1] = after[...].astype(jnp.float32)
        pad[1 : frames + 1, 1 : FH + 1] = x[...].astype(jnp.float32)
    tile = out.shape[-1]
    column = lax.broadcasted_iota(jnp.int32, (FH, FW, tile), 1)

    def mix(pad, taps, bias, k):
        sums = [None, None, None]
        for a in range(3):
            for b in range(3):
                slab = pad[k + a, b : b + FH]
                for e in range(3):
                    term = slab * taps[a * 9 + b * 3 + e : a * 9 + b * 3 + e + 1, :].reshape(1, 1, tile)
                    sums[e] = term if sums[e] is None else sums[e] + term
        lower = jnp.where(column > 0, pltpu.roll(sums[0], 1, 1), 0.0)
        upper = jnp.where(column < FW - 1, pltpu.roll(sums[2], FW - 1, 1), 0.0)
        return bias[...].reshape(1, 1, tile) + sums[1] + lower + upper

    @pl.loop(0, frames)
    def _(k):
        value = mix(pv, tv, cv, k)
        gate = mix(pg, tg, cg, k)
        out[k] = (value * (gate / (1.0 + jnp.exp(-gate)))).astype(out.dtype)


def conv_gate(grid, before, after, taps, bias):
    frames = grid.shape[0]
    part = grid.shape[-1] // 2
    tile = 128 if part % 128 == 0 else part
    operands, specs = [], []
    for x in (grid, before, after, taps, bias):
        lead = (0,) * (x.ndim - 1)
        for j in (0, 1):
            shift = j * part // tile if tile < part else 0
            operands.append(x if tile < part else x[..., j * part : (j + 1) * part])
            specs.append(pl.BlockSpec(x.shape[:-1] + (tile,), lambda i, lead=lead, shift=shift: lead + (i + shift,)))
    return pl.pallas_call(
        convolve,
        grid=(part // tile,),
        out_shape=jax.ShapeDtypeStruct((frames, FH, FW, part), jnp.bfloat16),
        in_specs=specs,
        out_specs=pl.BlockSpec((frames, FH, FW, tile), lambda i: (0, 0, 0, i)),
        scratch_shapes=[pltpu.VMEM((frames + 2, FH + 2, FW, tile), jnp.float32)] * 2,
        compiler_params=pltpu.CompilerParams(vmem_limit_bytes=40 * 1024 * 1024),
        name="conv_gate",
    )(*operands)


def shards(queries, key_rows, value_rows, retention, up_weight, conv_weight, conv_bias):
    normed, flat_weight = gather_and_attend(queries, key_rows, value_rows, retention, up_weight)
    groups = lax.axis_size("grp")
    core = lax.axis_index("grp") % 2
    up_vals = jnp.dot(normed, flat_weight, preferred_element_type=jnp.float32)
    up_vals = up_vals.astype(jnp.bfloat16)
    part = flat_weight.shape[1] // 2
    frames = up_vals.shape[0] // (FH * FW)
    grid = up_vals.reshape(frames, FH, FW, 2 * part)
    onward = [(i, i + 2) for i in range(groups - 2)]
    before = lax.ppermute(grid[-1:], "grp", onward)
    after = lax.ppermute(grid[:1], "grp", [(j, i) for i, j in onward])
    taps = lax.dynamic_slice_in_dim(conv_weight, core * part, part, axis=4)
    convolution_kernel = taps.reshape(27, 2 * part).astype(jnp.float32)
    bias = lax.dynamic_slice_in_dim(conv_bias, core * part, part, axis=1)
    hidden = conv_gate(grid, before, after, convolution_kernel, bias.reshape(1, 2 * part))
    hidden = hidden.reshape(2, frames * FH * FW // 2, part)
    mine = lax.dynamic_index_in_dim(hidden, core, 0, False)
    theirs = swap(lax.dynamic_index_in_dim(hidden, 1 - core, 0, False), groups)
    first = jnp.where(core == 0, mine, theirs)
    second = jnp.where(core == 0, theirs, mine)
    return jnp.concatenate([first, second], axis=1)


def solution(mesh):
    in_specs = (
        P(("grp", "span"), None),
        P(("grp", "span"), None),
        P(("grp", "span"), None),
        P(("grp", "span"), None),
        P("grp", None, "span"),
        P(None, None, None, None, "span"),
        P(None, "span"),
    )
    out_specs = P("grp", "span")
    return jax.shard_map(shards, mesh=mesh, in_specs=in_specs, out_specs=out_specs, check_vma=False)
```

```python
import functools

import jax
import jax.numpy as jnp
from jax import lax
from jax.experimental import pallas as pl
from jax.experimental.pallas import tpu as pltpu
from jax.sharding import PartitionSpec as P

FH = 8
FW = 16
BLOCK = 8
MESH = pl.DeviceIdType.MESH


def swap(x, groups):
    return lax.ppermute(x, "grp", [(i, i ^ 1) for i in range(groups)])


def fused(groups, members, heads, head_dim, kt_ref, v_ref, q_ref, ret_ref, w_ref, wg_ref, nrm_ref,
          local, outbox, inbox, tot_out, tot_in, back_out, back_in, within, attend, normed,
          s1, r1, s2, r2, s3, r3, sw, rw, sx, rx, sn, rn, sc, rc, se, re, st, rt, lsem):
    grp = lax.axis_index("grp")
    span = lax.axis_index("span")
    me = grp * members + span
    spot = me % BLOCK
    layer = me // BLOCK
    layers = groups * members // BLOCK
    core = grp % 2
    chip = grp // 2
    chips = groups // 2
    rows = heads * head_dim // BLOCK

    def device(r):
        return (r // members, r % members)

    even = chip % 2 == 0
    place = jnp.where(even, chip // 2, chips - 1 - chip // 2)

    def chip_at(p):
        p = (p + chips) % chips
        return jnp.where(p < chips // 2, 2 * p, 2 * (chips - 1 - p) + 1)

    right = (2 * chip_at(place + 1) + core, span)
    left = (2 * chip_at(place - 1) + core, span)
    twin = (2 * chip + 1 - core, span)
    mates = [(spot + k) % BLOCK for k in range(1, BLOCK)]
    others = [(layer + k) % layers for k in range(1, layers)]

    barrier = pltpu.get_barrier_semaphore()
    targets = [device(layer * BLOCK + m) for m in mates]
    targets += [device(o * BLOCK + spot) for o in others]
    targets += [right, left, twin]
    targets += [(2 * ((chip + 1) % chips) + core, span), (2 * ((chip + chips - 1) % chips) + core, span)]
    for t in targets:
        pl.semaphore_signal(barrier, inc=1, device_id=t, device_id_type=MESH)
    pl.semaphore_wait(barrier, len(targets))

    def send(src, dst, ssem, rsem, to):
        return pltpu.make_async_remote_copy(
            src_ref=src, dst_ref=dst, send_sem=ssem, recv_sem=rsem, device_id=to, device_id_type=MESH
        )

    across = send(w_ref.at[1 - core], wg_ref.at[chip, core], sx, rx, twin)
    across.start()
    keep = pltpu.make_async_copy(w_ref.at[core], wg_ref.at[chip, core], lsem.at[0])
    keep.start()

    half = chips // 2

    def halves(way, hop):
        if hop == half - 1:
            return (way,)
        return (0, 1)

    def hop_copy(way, hop, part):
        source = chip_at(place - hop) if way == 0 else chip_at(place + hop)
        at = wg_ref.at[source, (core + part) % 2]
        origin = w_ref.at[core] if hop == 0 and part == 0 else at
        return send(origin, at, sw.at[way, hop, part], rw.at[way, hop, part], right if way == 0 else left)

    def hop_wait(way, hop, part):
        source = chip_at(place - hop - 1) if way == 0 else chip_at(place + hop + 1)
        at = wg_ref.at[source, (core + part) % 2]
        send(at, at, sw.at[way, hop, part], rw.at[way, hop, part], right if way == 0 else left).wait_recv()

    started = []

    def launch(part):
        for way in (0, 1):
            if part in halves(way, 0):
                c = hop_copy(way, 0, part)
                c.start()
                started.append(c)

    launch(0)

    def slot(c, p):
        return nrm_ref.at[1 + c * members + p]

    steps = [(hop, part) for hop in range(1, half + 1) for part in (0, 1)]

    def ring(count):
        for _ in range(min(count, len(steps))):
            hop, part = steps.pop(0)
            for way in (0, 1):
                if part in halves(way, hop - 1):
                    hop_wait(way, hop - 1, part)
                if hop < half and part in halves(way, hop):
                    c = hop_copy(way, hop, part)
                    c.start()
                    started.append(c)

    lane = lax.broadcasted_iota(jnp.int32, (head_dim, 128), 1)
    for h in range(heads):
        if h == 2:
            across.wait()
            launch(1)
        state = jnp.dot(kt_ref[h], v_ref[h], preferred_element_type=jnp.float32)
        keepf = jnp.full((head_dim, 128), ret_ref[0, h], jnp.float32)
        high = keepf.astype(jnp.bfloat16).astype(jnp.float32)
        state = jnp.where(lane == head_dim + 1, high, state)
        state = jnp.where(lane == head_dim + 2, keepf - high, state)
        local[h * head_dim : (h + 1) * head_dim, :] = state
    for j in range(BLOCK):
        outbox[j] = local[j * rows : (j + 1) * rows, :].astype(jnp.bfloat16)
    pltpu.make_async_copy(outbox.at[spot], inbox.at[spot], lsem.at[1]).start()
    first = [
        send(outbox.at[m], inbox.at[spot], s1.at[m], r1.at[spot], device(layer * BLOCK + m)) for m in mates
    ]
    for c in first:
        c.start()

    pltpu.make_async_copy(outbox.at[spot], inbox.at[spot], lsem.at[1]).wait()
    for m in mates:
        send(outbox.at[m], inbox.at[m], s1.at[m], r1.at[m], device(layer * BLOCK + m)).wait_recv()
    wide = lax.broadcasted_iota(jnp.int32, (rows, 128), 1)

    def factor_of(x):
        return x[:, head_dim + 1 : head_dim + 2] + x[:, head_dim + 2 : head_dim + 3]

    running = jnp.zeros((rows, 128), jnp.float32)
    factor = jnp.ones((rows, 1), jnp.float32)
    factors = []
    for j in range(BLOCK):
        within[j] = running
        factors.append(factor)
        got = inbox[j].astype(jnp.float32)
        f = factor_of(got)
        running = f * running + got
        factor = factor * f
    full = jnp.broadcast_to(factor, (rows, 128))
    high = full.astype(jnp.bfloat16).astype(jnp.float32)
    total = jnp.where(wide == head_dim + 1, high, running)
    total = jnp.where(wide == head_dim + 2, full - high, total)
    tot_out[...] = total.astype(jnp.bfloat16)
    second = [
        send(tot_out, tot_in.at[layer], s2.at[o], r2.at[layer], device(o * BLOCK + spot)) for o in others
    ]
    for c in second:
        c.start()
    ring(1)
    for o in others:
        send(tot_out, tot_in.at[o], s2.at[o], r2.at[o], device(o * BLOCK + spot)).wait_recv()

    def earlier(i, carry):
        got = tot_in[i].astype(jnp.float32)
        return factor_of(got) * carry + got

    before = lax.fori_loop(0, layer, earlier, jnp.zeros((rows, 128), jnp.float32))
    for j in range(BLOCK):
        back_out[j] = (factors[j] * before + within[j]).astype(jnp.bfloat16)
    pltpu.make_async_copy(back_out.at[spot], back_in.at[spot], lsem.at[2]).start()
    third = [
        send(back_out.at[m], back_in.at[spot], s3.at[m], r3.at[spot], device(layer * BLOCK + m)) for m in mates
    ]
    for c in third:
        c.start()
    ring(1)
    pltpu.make_async_copy(back_out.at[spot], back_in.at[spot], lsem.at[2]).wait()
    for m in mates:
        send(back_out.at[m], back_in.at[m], s3.at[m], r3.at[m], device(layer * BLOCK + m)).wait_recv()
    for j in range(BLOCK):
        part = slice(j * rows, (j + 1) * rows)
        got = local[part, :]
        local[part, :] = factor_of(got) * back_in[j].astype(jnp.float32) + got

    ring(1)
    tokens = q_ref.shape[1]
    cut = heads * head_dim // groups
    depth = w_ref.shape[1]
    attend[...] = jnp.zeros_like(attend)
    squares = jnp.zeros((q_ref.shape[1], 1), jnp.float32)
    column = lax.broadcasted_iota(jnp.int32, (q_ref.shape[1], 128), 1)
    for h in range(heads):
        state = local[h * head_dim : (h + 1) * head_dim, :].astype(jnp.bfloat16)
        numer = jnp.dot(q_ref[h], state, preferred_element_type=jnp.float32)
        value = numer / (numer[:, head_dim : head_dim + 1] + 0.0001)
        value = jnp.where(column < head_dim, value, 0.0)
        squares = squares + jnp.sum(value * value, axis=1, keepdims=True)
        at, stop = h * head_dim, (h + 1) * head_dim
        while at < stop:
            block = at // cut
            end = min(stop, (block + 1) * cut)
            to = block * depth + at - block * cut
            attend[:, to : to + end - at] = value[:, at - h * head_dim : end - h * head_dim]
            at = end
    ring(1)
    scale = lax.rsqrt(squares / (heads * head_dim) + 1e-06)
    normed[...] = (attend[...] * scale).astype(jnp.bfloat16)
    keepn = pltpu.make_async_copy(normed, slot(core, span), lsem.at[3])
    keepn.start()
    peers = [(span + k) % members for k in range(1, members)]
    fourth = [
        send(normed, slot(core, span), sn.at[p], rn.at[span], (grp, p)) for p in peers
    ]
    for c in fourth:
        c.start()
    cross = [send(normed, slot(core, span), sc.at[span], rc.at[span], twin)]
    cross[0].start()
    ring(2)
    for p in peers:
        send(normed, slot(core, p), sn.at[p], rn.at[p], (grp, p)).wait_recv()
        c = send(slot(core, p), slot(core, p), sc.at[p], rc.at[p], twin)
        c.start()
        cross.append(c)
    keepn.wait()
    for p in [span] + peers:
        send(slot(1 - core, p), slot(1 - core, p), sc.at[p], rc.at[p], twin).wait_recv()

    middle = tokens // 2
    has = (chip > 0, chip < chips - 1)

    def edge(side, part):
        return nrm_ref.at[side * (2 * members + 1), pl.ds(pl.multiple_of(part * middle, middle), middle)]

    def edge_copy(side):
        source = nrm_ref.at[
            2 * members if side == 0 else 1, pl.ds(pl.multiple_of(core * middle, middle), middle)
        ]
        target = (2 * (chip + (1 if side == 0 else -1)) + core, span)
        return send(source, edge(side, core), se.at[side], re.at[side], target)

    def twin_copy(side, part):
        return send(edge(side, part), edge(side, part), st.at[side], rt.at[side], twin)

    for side in (0, 1):
        @pl.when(has[1 - side])
        def _(side=side):
            edge_copy(side).start()

    for side in (0, 1):
        @pl.when(has[side])
        def _(side=side):
            edge_copy(side).wait_recv()
            twin_copy(side, core).start()

    ring(len(steps))
    for side in (0, 1):
        @pl.when(has[side])
        def _(side=side):
            twin_copy(side, 1 - core).wait_recv()
            twin_copy(side, core).wait_send()

        @pl.when(has[1 - side])
        def _(side=side):
            edge_copy(side).wait_send()

    keep.wait()
    for c in first + second + third + fourth + cross + started:
        c.wait_send()


def gather_and_attend(queries, key_rows, value_rows, retention, up_weight):
    groups = lax.axis_size("grp")
    members = lax.axis_size("span")
    tokens, dim = queries.shape
    heads = retention.shape[1]
    head_dim = dim // heads
    rows, _, width = up_weight.shape
    part = width // 2
    depth = -(-rows // 16) * 16
    kt = jnp.maximum(key_rows, 0).T.reshape(heads, head_dim, tokens)
    q = jnp.maximum(queries, 0).reshape(tokens, heads, head_dim).transpose(1, 0, 2)
    v = value_rows.reshape(tokens, heads, head_dim).transpose(1, 0, 2)
    rest = 128 - head_dim
    one = jnp.ones((heads, tokens, 1), v.dtype)
    v = jnp.concatenate([v, one, jnp.zeros((heads, tokens, rest - 1), v.dtype)], axis=2)
    w = up_weight.reshape(rows, 2, 2, part).transpose(2, 0, 1, 3).reshape(2, rows, width)
    w = jnp.pad(w, ((0, 0), (0, depth - rows), (0, 0)))
    chips = groups // 2
    share = dim // BLOCK
    layers = groups * members // BLOCK
    dma = pltpu.SemaphoreType.DMA
    vmem = pl.BlockSpec(memory_space=pltpu.VMEM)
    anywhere = pl.BlockSpec(memory_space=pl.ANY)
    bf = jnp.bfloat16
    slabs = pltpu.VMEM((BLOCK, share, 128), bf)
    weight, normed = pl.pallas_call(
        functools.partial(fused, groups, members, heads, head_dim),
        out_shape=(
            jax.ShapeDtypeStruct((chips, 2, depth, width), bf),
            jax.ShapeDtypeStruct((2 * members + 2, tokens, groups * depth), bf),
        ),
        in_specs=[vmem, vmem, vmem, pl.BlockSpec(memory_space=pltpu.SMEM), anywhere],
        out_specs=(anywhere, anywhere),
        scratch_shapes=[
            pltpu.VMEM((dim, 128), jnp.float32),
            slabs,
            slabs,
            pltpu.VMEM((share, 128), bf),
            pltpu.VMEM((layers, share, 128), bf),
            slabs,
            slabs,
            pltpu.VMEM((BLOCK, share, 128), jnp.float32),
            pltpu.VMEM((tokens, groups * depth), jnp.float32),
            pltpu.VMEM((tokens, groups * depth), bf),
            dma((BLOCK,)), dma((BLOCK,)),
            dma((layers,)), dma((layers,)),
            dma((BLOCK,)), dma((BLOCK,)),
            dma((2, chips // 2, 2)), dma((2, chips // 2, 2)),
            dma, dma,
            dma((members,)), dma((members,)),
            dma((members,)), dma((members,)),
            dma((2,)), dma((2,)),
            dma((2,)), dma((2,)),
            dma((4,)),
        ],
        compiler_params=pltpu.CompilerParams(
            collective_id=0, has_side_effects=True, vmem_limit_bytes=32 * 1024 * 1024
        ),
        name="gather_and_attend",
    )(kt, v, q, retention, w)
    weight = weight.reshape(groups * depth, width)
    return normed.reshape((2 * members + 2) * tokens, groups * depth), weight


def convolve(edges, xv, xg, tv, tg, cv, cg, out, pv, pg):
    frames = out.shape[0]
    for x, pad in ((xv, pv), (xg, pg)):
        pad[:, 0:1] = jnp.zeros_like(pad[:, 0:1])
        pad[:, FH + 1 :] = jnp.zeros_like(pad[:, FH + 1 :])
        pad[1 : frames + 1, 1 : FH + 1] = x[1 : frames + 1].astype(jnp.float32)
        for side, k in ((0, 0), (1, frames + 1)):
            pad[k, 1 : FH + 1] = jnp.where(edges[0, side] > 0, x[k].astype(jnp.float32), 0.0)
    tile = out.shape[-1]
    column = lax.broadcasted_iota(jnp.int32, (FH, FW, tile), 1)

    def mix(pad, taps, bias, k):
        sums = [None, None, None]
        for a in range(3):
            for b in range(3):
                slab = pad[k + a, b : b + FH]
                for e in range(3):
                    term = slab * taps[a * 9 + b * 3 + e : a * 9 + b * 3 + e + 1, :].reshape(1, 1, tile)
                    sums[e] = term if sums[e] is None else sums[e] + term
        lower = jnp.where(column > 0, pltpu.roll(sums[0], 1, 1), 0.0)
        upper = jnp.where(column < FW - 1, pltpu.roll(sums[2], FW - 1, 1), 0.0)
        return bias[...].reshape(1, 1, tile) + sums[1] + lower + upper

    @pl.loop(0, frames)
    def _(k):
        value = mix(pv, tv, cv, k)
        gate = mix(pg, tg, cg, k)
        out[k] = (value * (gate / (1.0 + jnp.exp(-gate)))).astype(out.dtype)


def conv_gate(edges, grid, taps, bias):
    frames = grid.shape[0] - 2
    part = grid.shape[-1] // 2
    tile = 128 if part % 128 == 0 else part
    operands, specs = [edges], [pl.BlockSpec(memory_space=pltpu.SMEM)]
    for x in (grid, taps, bias):
        lead = (0,) * (x.ndim - 1)
        for j in (0, 1):
            shift = j * part // tile if tile < part else 0
            operands.append(x if tile < part else x[..., j * part : (j + 1) * part])
            specs.append(pl.BlockSpec(x.shape[:-1] + (tile,), lambda i, lead=lead, shift=shift: lead + (i + shift,)))
    return pl.pallas_call(
        convolve,
        grid=(part // tile,),
        out_shape=jax.ShapeDtypeStruct((frames, FH, FW, part), jnp.bfloat16),
        in_specs=specs,
        out_specs=pl.BlockSpec((frames, FH, FW, tile), lambda i: (0, 0, 0, i)),
        scratch_shapes=[pltpu.VMEM((frames + 2, FH + 2, FW, tile), jnp.float32)] * 2,
        compiler_params=pltpu.CompilerParams(vmem_limit_bytes=40 * 1024 * 1024),
        name="conv_gate",
    )(*operands)


def shards(queries, key_rows, value_rows, retention, up_weight, conv_weight, conv_bias):
    normed, flat_weight = gather_and_attend(queries, key_rows, value_rows, retention, up_weight)
    groups = lax.axis_size("grp")
    core = lax.axis_index("grp") % 2
    up_vals = jnp.dot(normed, flat_weight, preferred_element_type=jnp.float32)
    up_vals = up_vals.astype(jnp.bfloat16)
    part = flat_weight.shape[1] // 2
    frames = up_vals.shape[0] // (FH * FW) - 2
    grid = up_vals.reshape(frames + 2, FH, FW, 2 * part)
    group = lax.axis_index("grp")
    edges = jnp.stack([group >= 2, group < groups - 2]).astype(jnp.int32).reshape(1, 2)
    taps = lax.dynamic_slice_in_dim(conv_weight, core * part, part, axis=4)
    convolution_kernel = taps.reshape(27, 2 * part).astype(jnp.float32)
    bias = lax.dynamic_slice_in_dim(conv_bias, core * part, part, axis=1)
    hidden = conv_gate(edges, grid, convolution_kernel, bias.reshape(1, 2 * part))
    hidden = hidden.reshape(2, frames * FH * FW // 2, part)
    mine = lax.dynamic_index_in_dim(hidden, core, 0, False)
    theirs = swap(lax.dynamic_index_in_dim(hidden, 1 - core, 0, False), groups)
    first = jnp.where(core == 0, mine, theirs)
    second = jnp.where(core == 0, theirs, mine)
    return jnp.concatenate([first, second], axis=1)


def solution(mesh):
    in_specs = (
        P(("grp", "span"), None),
        P(("grp", "span"), None),
        P(("grp", "span"), None),
        P(("grp", "span"), None),
        P("grp", None, "span"),
        P(None, None, None, None, "span"),
        P(None, "span"),
    )
    out_specs = P("grp", "span")
    return jax.shard_map(shards, mesh=mesh, in_specs=in_specs, out_specs=out_specs, check_vma=False)
```

```python
import functools

import jax
import jax.numpy as jnp
from jax import lax
from jax.experimental import pallas as pl
from jax.experimental.pallas import tpu as pltpu
from jax.sharding import PartitionSpec as P

FH = 8
FW = 16
BLOCK = 8
MESH = pl.DeviceIdType.MESH


def swap(x, groups):
    return lax.ppermute(x, "grp", [(i, i ^ 1) for i in range(groups)])


def fused(groups, members, heads, head_dim, kt_ref, v_ref, q_ref, ret_ref, w_ref, wg_ref, nrm_ref,
          local, outbox, inbox, tot_out, tot_in, back_out, back_in, within, attend, normed,
          s1, r1, s2, r2, s3, r3, sw, rw, sx, rx, sn, rn, sc, rc, se, re, st, rt, lsem):
    grp = lax.axis_index("grp")
    span = lax.axis_index("span")
    me = grp * members + span
    spot = me % BLOCK
    layer = me // BLOCK
    layers = groups * members // BLOCK
    core = grp % 2
    chip = grp // 2
    chips = groups // 2
    rows = heads * head_dim // BLOCK

    def device(r):
        return (r // members, r % members)

    even = chip % 2 == 0
    place = jnp.where(even, chip // 2, chips - 1 - chip // 2)

    def chip_at(p):
        p = (p + chips) % chips
        return jnp.where(p < chips // 2, 2 * p, 2 * (chips - 1 - p) + 1)

    right = (2 * chip_at(place + 1) + core, span)
    left = (2 * chip_at(place - 1) + core, span)
    twin = (2 * chip + 1 - core, span)
    mates = [(spot + k) % BLOCK for k in range(1, BLOCK)]
    others = [(layer + k) % layers for k in range(1, layers)]

    barrier = pltpu.get_barrier_semaphore()
    targets = [device(layer * BLOCK + m) for m in mates]
    targets += [device(o * BLOCK + spot) for o in others]
    targets += [right, left, twin]
    targets += [(2 * ((chip + 1) % chips) + core, span), (2 * ((chip + chips - 1) % chips) + core, span)]
    for t in targets:
        pl.semaphore_signal(barrier, inc=1, device_id=t, device_id_type=MESH)
    pl.semaphore_wait(barrier, len(targets))

    def send(src, dst, ssem, rsem, to):
        return pltpu.make_async_remote_copy(
            src_ref=src, dst_ref=dst, send_sem=ssem, recv_sem=rsem, device_id=to, device_id_type=MESH
        )

    across = send(w_ref.at[1 - core], wg_ref.at[chip, core], sx, rx, twin)
    across.start()
    keep = pltpu.make_async_copy(w_ref.at[core], wg_ref.at[chip, core], lsem.at[0])
    keep.start()

    half = chips // 2

    def halves(way, hop):
        if hop == half - 1:
            return (way,)
        return (0, 1)

    def hop_copy(way, hop, part):
        source = chip_at(place - hop) if way == 0 else chip_at(place + hop)
        at = wg_ref.at[source, (core + part) % 2]
        origin = w_ref.at[core] if hop == 0 and part == 0 else at
        return send(origin, at, sw.at[way, hop, part], rw.at[way, hop, part], right if way == 0 else left)

    def hop_wait(way, hop, part):
        source = chip_at(place - hop - 1) if way == 0 else chip_at(place + hop + 1)
        at = wg_ref.at[source, (core + part) % 2]
        send(at, at, sw.at[way, hop, part], rw.at[way, hop, part], right if way == 0 else left).wait_recv()

    started = []

    def launch(part):
        for way in (0, 1):
            if part in halves(way, 0):
                c = hop_copy(way, 0, part)
                c.start()
                started.append(c)

    launch(0)

    def slot(c, p):
        return nrm_ref.at[1 + c * members + p]

    steps = [(hop, part) for hop in range(1, half + 1) for part in (0, 1)]

    def ring(count):
        for _ in range(min(count, len(steps))):
            hop, part = steps.pop(0)
            for way in (0, 1):
                if part in halves(way, hop - 1):
                    hop_wait(way, hop - 1, part)
                if hop < half and part in halves(way, hop):
                    c = hop_copy(way, hop, part)
                    c.start()
                    started.append(c)

    lane = lax.broadcasted_iota(jnp.int32, (head_dim, 128), 1)
    for h in range(heads):
        if h == 2:
            across.wait()
            launch(1)
        state = jnp.dot(kt_ref[h], v_ref[h], preferred_element_type=jnp.float32)
        keepf = jnp.full((head_dim, 128), ret_ref[0, h], jnp.float32)
        high = keepf.astype(jnp.bfloat16).astype(jnp.float32)
        state = jnp.where(lane == head_dim + 1, high, state)
        state = jnp.where(lane == head_dim + 2, keepf - high, state)
        local[h * head_dim : (h + 1) * head_dim, :] = state
    for j in range(BLOCK):
        outbox[j] = local[j * rows : (j + 1) * rows, :].astype(jnp.bfloat16)
    pltpu.make_async_copy(outbox.at[spot], inbox.at[spot], lsem.at[1]).start()
    first = [
        send(outbox.at[m], inbox.at[spot], s1.at[m], r1.at[spot], device(layer * BLOCK + m)) for m in mates
    ]
    for c in first:
        c.start()

    pltpu.make_async_copy(outbox.at[spot], inbox.at[spot], lsem.at[1]).wait()
    for m in mates:
        send(outbox.at[m], inbox.at[m], s1.at[m], r1.at[m], device(layer * BLOCK + m)).wait_recv()
    wide = lax.broadcasted_iota(jnp.int32, (rows, 128), 1)

    def factor_of(x):
        return x[:, head_dim + 1 : head_dim + 2] + x[:, head_dim + 2 : head_dim + 3]

    running = jnp.zeros((rows, 128), jnp.float32)
    factor = jnp.ones((rows, 1), jnp.float32)
    factors = []
    for j in range(BLOCK):
        within[j] = running
        factors.append(factor)
        got = inbox[j].astype(jnp.float32)
        f = factor_of(got)
        running = f * running + got
        factor = factor * f
    full = jnp.broadcast_to(factor, (rows, 128))
    high = full.astype(jnp.bfloat16).astype(jnp.float32)
    total = jnp.where(wide == head_dim + 1, high, running)
    total = jnp.where(wide == head_dim + 2, full - high, total)
    tot_out[...] = total.astype(jnp.bfloat16)
    second = [
        send(tot_out, tot_in.at[layer], s2.at[o], r2.at[layer], device(o * BLOCK + spot)) for o in others
    ]
    for c in second:
        c.start()
    ring(1)
    for o in others:
        send(tot_out, tot_in.at[o], s2.at[o], r2.at[o], device(o * BLOCK + spot)).wait_recv()

    def earlier(i, carry):
        got = tot_in[i].astype(jnp.float32)
        return factor_of(got) * carry + got

    before = lax.fori_loop(0, layer, earlier, jnp.zeros((rows, 128), jnp.float32))
    for j in range(BLOCK):
        back_out[j] = (factors[j] * before + within[j]).astype(jnp.bfloat16)
    pltpu.make_async_copy(back_out.at[spot], back_in.at[spot], lsem.at[2]).start()
    third = [
        send(back_out.at[m], back_in.at[spot], s3.at[m], r3.at[spot], device(layer * BLOCK + m)) for m in mates
    ]
    for c in third:
        c.start()
    ring(1)
    pltpu.make_async_copy(back_out.at[spot], back_in.at[spot], lsem.at[2]).wait()
    for m in mates:
        send(back_out.at[m], back_in.at[m], s3.at[m], r3.at[m], device(layer * BLOCK + m)).wait_recv()
    for j in range(BLOCK):
        part = slice(j * rows, (j + 1) * rows)
        got = local[part, :]
        local[part, :] = factor_of(got) * back_in[j].astype(jnp.float32) + got

    ring(1)
    tokens = q_ref.shape[1]
    cut = heads * head_dim // groups
    depth = w_ref.shape[1]
    attend[...] = jnp.zeros_like(attend)
    squares = jnp.zeros((q_ref.shape[1], 1), jnp.float32)
    column = lax.broadcasted_iota(jnp.int32, (q_ref.shape[1], 128), 1)
    for h in range(heads):
        state = local[h * head_dim : (h + 1) * head_dim, :].astype(jnp.bfloat16)
        numer = jnp.dot(q_ref[h], state, preferred_element_type=jnp.float32)
        value = numer / (numer[:, head_dim : head_dim + 1] + 0.0001)
        value = jnp.where(column < head_dim, value, 0.0)
        squares = squares + jnp.sum(value * value, axis=1, keepdims=True)
        at, stop = h * head_dim, (h + 1) * head_dim
        while at < stop:
            block = at // cut
            end = min(stop, (block + 1) * cut)
            to = block * depth + at - block * cut
            attend[:, to : to + end - at] = value[:, at - h * head_dim : end - h * head_dim]
            at = end
    ring(1)
    scale = lax.rsqrt(squares / (heads * head_dim) + 1e-06)
    normed[...] = (attend[...] * scale).astype(jnp.bfloat16)
    keepn = pltpu.make_async_copy(normed, slot(core, span), lsem.at[3])
    keepn.start()
    peers = [(span + k) % members for k in range(1, members)]
    fourth = [
        send(normed, slot(core, span), sn.at[p], rn.at[span], (grp, p)) for p in peers
    ]
    for c in fourth:
        c.start()
    cross = [send(normed, slot(core, span), sc.at[span], rc.at[span], twin)]
    cross[0].start()
    ring(1)
    for p in peers:
        send(normed, slot(core, p), sn.at[p], rn.at[p], (grp, p)).wait_recv()
        c = send(slot(core, p), slot(core, p), sc.at[p], rc.at[p], twin)
        c.start()
        cross.append(c)
    keepn.wait()
    for p in [span] + peers:
        send(slot(1 - core, p), slot(1 - core, p), sc.at[p], rc.at[p], twin).wait_recv()

    middle = tokens // 2
    has = (chip > 0, chip < chips - 1)

    def edge(side, part):
        return nrm_ref.at[side * (2 * members + 1), pl.ds(pl.multiple_of(part * middle, middle), middle)]

    def edge_copy(side):
        source = nrm_ref.at[
            2 * members if side == 0 else 1, pl.ds(pl.multiple_of(core * middle, middle), middle)
        ]
        target = (2 * (chip + (1 if side == 0 else -1)) + core, span)
        return send(source, edge(side, core), se.at[side], re.at[side], target)

    def twin_copy(side, part):
        return send(edge(side, part), edge(side, part), st.at[side], rt.at[side], twin)

    for side in (0, 1):
        @pl.when(has[1 - side])
        def _(side=side):
            edge_copy(side).start()

    ring(1)

    for side in (0, 1):
        @pl.when(has[side])
        def _(side=side):
            edge_copy(side).wait_recv()
            twin_copy(side, core).start()

    ring(len(steps))
    for side in (0, 1):
        @pl.when(has[side])
        def _(side=side):
            twin_copy(side, 1 - core).wait_recv()
            twin_copy(side, core).wait_send()

        @pl.when(has[1 - side])
        def _(side=side):
            edge_copy(side).wait_send()

    keep.wait()
    for c in first + second + third + fourth + cross + started:
        c.wait_send()


def gather_and_attend(queries, key_rows, value_rows, retention, up_weight):
    groups = lax.axis_size("grp")
    members = lax.axis_size("span")
    tokens, dim = queries.shape
    heads = retention.shape[1]
    head_dim = dim // heads
    rows, _, width = up_weight.shape
    part = width // 2
    depth = -(-rows // 16) * 16
    kt = jnp.maximum(key_rows, 0).T.reshape(heads, head_dim, tokens)
    q = jnp.maximum(queries, 0).reshape(tokens, heads, head_dim).transpose(1, 0, 2)
    v = value_rows.reshape(tokens, heads, head_dim).transpose(1, 0, 2)
    rest = 128 - head_dim
    one = jnp.ones((heads, tokens, 1), v.dtype)
    v = jnp.concatenate([v, one, jnp.zeros((heads, tokens, rest - 1), v.dtype)], axis=2)
    w = up_weight.reshape(rows, 2, 2, part).transpose(2, 0, 1, 3).reshape(2, rows, width)
    w = jnp.pad(w, ((0, 0), (0, depth - rows), (0, 0)))
    chips = groups // 2
    share = dim // BLOCK
    layers = groups * members // BLOCK
    dma = pltpu.SemaphoreType.DMA
    vmem = pl.BlockSpec(memory_space=pltpu.VMEM)
    anywhere = pl.BlockSpec(memory_space=pl.ANY)
    bf = jnp.bfloat16
    slabs = pltpu.VMEM((BLOCK, share, 128), bf)
    weight, normed = pl.pallas_call(
        functools.partial(fused, groups, members, heads, head_dim),
        out_shape=(
            jax.ShapeDtypeStruct((chips, 2, depth, width), bf),
            jax.ShapeDtypeStruct((2 * members + 2, tokens, groups * depth), bf),
        ),
        in_specs=[vmem, vmem, vmem, pl.BlockSpec(memory_space=pltpu.SMEM), anywhere],
        out_specs=(anywhere, anywhere),
        scratch_shapes=[
            pltpu.VMEM((dim, 128), jnp.float32),
            slabs,
            slabs,
            pltpu.VMEM((share, 128), bf),
            pltpu.VMEM((layers, share, 128), bf),
            slabs,
            slabs,
            pltpu.VMEM((BLOCK, share, 128), jnp.float32),
            pltpu.VMEM((tokens, groups * depth), jnp.float32),
            pltpu.VMEM((tokens, groups * depth), bf),
            dma((BLOCK,)), dma((BLOCK,)),
            dma((layers,)), dma((layers,)),
            dma((BLOCK,)), dma((BLOCK,)),
            dma((2, chips // 2, 2)), dma((2, chips // 2, 2)),
            dma, dma,
            dma((members,)), dma((members,)),
            dma((members,)), dma((members,)),
            dma((2,)), dma((2,)),
            dma((2,)), dma((2,)),
            dma((4,)),
        ],
        compiler_params=pltpu.CompilerParams(
            collective_id=0, has_side_effects=True, vmem_limit_bytes=32 * 1024 * 1024
        ),
        name="gather_and_attend",
    )(kt, v, q, retention, w)
    weight = weight.reshape(groups * depth, width)
    return normed.reshape((2 * members + 2) * tokens, groups * depth), weight


def convolve(edges, xv, xg, tv, tg, cv, cg, out, pv, pg):
    frames = out.shape[0]
    for x, pad in ((xv, pv), (xg, pg)):
        pad[:, 0:1] = jnp.zeros_like(pad[:, 0:1])
        pad[:, FH + 1 :] = jnp.zeros_like(pad[:, FH + 1 :])
        pad[1 : frames + 1, 1 : FH + 1] = x[1 : frames + 1].astype(jnp.float32)
        for side, k in ((0, 0), (1, frames + 1)):
            pad[k, 1 : FH + 1] = jnp.where(edges[0, side] > 0, x[k].astype(jnp.float32), 0.0)
    tile = out.shape[-1]
    column = lax.broadcasted_iota(jnp.int32, (FH, FW, tile), 1)

    def mix(pad, taps, bias, k):
        sums = [None, None, None]
        for a in range(3):
            for b in range(3):
                slab = pad[k + a, b : b + FH]
                for e in range(3):
                    term = slab * taps[a * 9 + b * 3 + e : a * 9 + b * 3 + e + 1, :].reshape(1, 1, tile)
                    sums[e] = term if sums[e] is None else sums[e] + term
        lower = jnp.where(column > 0, pltpu.roll(sums[0], 1, 1), 0.0)
        upper = jnp.where(column < FW - 1, pltpu.roll(sums[2], FW - 1, 1), 0.0)
        return bias[...].reshape(1, 1, tile) + sums[1] + lower + upper

    @pl.loop(0, frames)
    def _(k):
        value = mix(pv, tv, cv, k)
        gate = mix(pg, tg, cg, k)
        out[k] = (value * (gate / (1.0 + jnp.exp(-gate)))).astype(out.dtype)


def conv_gate(edges, grid, taps, bias):
    frames = grid.shape[0] - 2
    part = grid.shape[-1] // 2
    tile = 256 if part % 256 == 0 else 128 if part % 128 == 0 else part
    operands, specs = [edges], [pl.BlockSpec(memory_space=pltpu.SMEM)]
    for x in (grid, taps, bias):
        lead = (0,) * (x.ndim - 1)
        for j in (0, 1):
            shift = j * part // tile if tile < part else 0
            operands.append(x if tile < part else x[..., j * part : (j + 1) * part])
            specs.append(pl.BlockSpec(x.shape[:-1] + (tile,), lambda i, lead=lead, shift=shift: lead + (i + shift,)))
    return pl.pallas_call(
        convolve,
        grid=(part // tile,),
        out_shape=jax.ShapeDtypeStruct((frames, FH, FW, part), jnp.bfloat16),
        in_specs=specs,
        out_specs=pl.BlockSpec((frames, FH, FW, tile), lambda i: (0, 0, 0, i)),
        scratch_shapes=[pltpu.VMEM((frames + 2, FH + 2, FW, tile), jnp.float32)] * 2,
        compiler_params=pltpu.CompilerParams(vmem_limit_bytes=40 * 1024 * 1024),
        name="conv_gate",
    )(*operands)


def shards(queries, key_rows, value_rows, retention, up_weight, conv_weight, conv_bias):
    normed, flat_weight = gather_and_attend(queries, key_rows, value_rows, retention, up_weight)
    groups = lax.axis_size("grp")
    core = lax.axis_index("grp") % 2
    up_vals = jnp.dot(normed, flat_weight, preferred_element_type=jnp.float32)
    up_vals = up_vals.astype(jnp.bfloat16)
    part = flat_weight.shape[1] // 2
    frames = up_vals.shape[0] // (FH * FW) - 2
    grid = up_vals.reshape(frames + 2, FH, FW, 2 * part)
    group = lax.axis_index("grp")
    edges = jnp.stack([group >= 2, group < groups - 2]).astype(jnp.int32).reshape(1, 2)
    taps = lax.dynamic_slice_in_dim(conv_weight, core * part, part, axis=4)
    convolution_kernel = taps.reshape(27, 2 * part).astype(jnp.float32)
    bias = lax.dynamic_slice_in_dim(conv_bias, core * part, part, axis=1)
    hidden = conv_gate(edges, grid, convolution_kernel, bias.reshape(1, 2 * part))
    hidden = hidden.reshape(2, frames * FH * FW // 2, part)
    mine = lax.dynamic_index_in_dim(hidden, core, 0, False)
    theirs = swap(lax.dynamic_index_in_dim(hidden, 1 - core, 0, False), groups)
    first = jnp.where(core == 0, mine, theirs)
    second = jnp.where(core == 0, theirs, mine)
    return jnp.concatenate([first, second], axis=1)


def solution(mesh):
    in_specs = (
        P(("grp", "span"), None),
        P(("grp", "span"), None),
        P(("grp", "span"), None),
        P(("grp", "span"), None),
        P("grp", None, "span"),
        P(None, None, None, None, "span"),
        P(None, "span"),
    )
    out_specs = P("grp", "span")
    return jax.shard_map(shards, mesh=mesh, in_specs=in_specs, out_specs=out_specs, check_vma=False)
```

```python
import functools

import jax
import jax.numpy as jnp
from jax import lax
from jax.experimental import pallas as pl
from jax.experimental.pallas import tpu as pltpu
from jax.sharding import PartitionSpec as P

FH = 8
FW = 16
BLOCK = 8
MESH = pl.DeviceIdType.MESH


def swap(x, groups):
    return lax.ppermute(x, "grp", [(i, i ^ 1) for i in range(groups)])


def fused(groups, members, heads, head_dim, kt_ref, v_ref, q_ref, ret_ref, w_ref, wg_ref, nrm_ref,
          local, outbox, inbox, tot_out, tot_in, back_out, back_in, within, attend, normed,
          s1, r1, s2, r2, s3, r3, sw, rw, sx, rx, sn, rn, sc, rc, se, re, st, rt, lsem):
    grp = lax.axis_index("grp")
    span = lax.axis_index("span")
    me = grp * members + span
    spot = me % BLOCK
    layer = me // BLOCK
    layers = groups * members // BLOCK
    core = grp % 2
    chip = grp // 2
    chips = groups // 2
    rows = heads * head_dim // BLOCK

    def device(r):
        return (r // members, r % members)

    even = chip % 2 == 0
    place = jnp.where(even, chip // 2, chips - 1 - chip // 2)

    def chip_at(p):
        p = (p + chips) % chips
        return jnp.where(p < chips // 2, 2 * p, 2 * (chips - 1 - p) + 1)

    right = (2 * chip_at(place + 1) + core, span)
    left = (2 * chip_at(place - 1) + core, span)
    twin = (2 * chip + 1 - core, span)
    mates = [(spot + k) % BLOCK for k in range(1, BLOCK)]
    others = [(layer + k) % layers for k in range(1, layers)]

    barrier = pltpu.get_barrier_semaphore()
    targets = [device(layer * BLOCK + m) for m in mates]
    targets += [device(o * BLOCK + spot) for o in others]
    targets += [right, left, twin]
    targets += [(2 * ((chip + 1) % chips) + core, span), (2 * ((chip + chips - 1) % chips) + core, span)]
    for t in targets:
        pl.semaphore_signal(barrier, inc=1, device_id=t, device_id_type=MESH)
    pl.semaphore_wait(barrier, len(targets))

    def send(src, dst, ssem, rsem, to):
        return pltpu.make_async_remote_copy(
            src_ref=src, dst_ref=dst, send_sem=ssem, recv_sem=rsem, device_id=to, device_id_type=MESH
        )

    across = send(w_ref.at[1 - core], wg_ref.at[chip, core], sx, rx, twin)
    across.start()
    keep = pltpu.make_async_copy(w_ref.at[core], wg_ref.at[chip, core], lsem.at[0])
    keep.start()

    half = chips // 2

    def halves(way, hop):
        if hop == half - 1:
            return (way,)
        return (0, 1)

    def hop_copy(way, hop, part):
        source = chip_at(place - hop) if way == 0 else chip_at(place + hop)
        at = wg_ref.at[source, (core + part) % 2]
        origin = w_ref.at[core] if hop == 0 and part == 0 else at
        return send(origin, at, sw.at[way, hop, part], rw.at[way, hop, part], right if way == 0 else left)

    def hop_wait(way, hop, part):
        source = chip_at(place - hop - 1) if way == 0 else chip_at(place + hop + 1)
        at = wg_ref.at[source, (core + part) % 2]
        send(at, at, sw.at[way, hop, part], rw.at[way, hop, part], right if way == 0 else left).wait_recv()

    started = []

    def launch(part):
        for way in (0, 1):
            if part in halves(way, 0):
                c = hop_copy(way, 0, part)
                c.start()
                started.append(c)

    launch(0)

    def slot(c, p):
        return nrm_ref.at[1 + c * members + p]

    steps = [(hop, part) for hop in range(1, half + 1) for part in (0, 1)]

    def ring(count):
        for _ in range(min(count, len(steps))):
            hop, part = steps.pop(0)
            for way in (0, 1):
                if part in halves(way, hop - 1):
                    hop_wait(way, hop - 1, part)
                if hop < half and part in halves(way, hop):
                    c = hop_copy(way, hop, part)
                    c.start()
                    started.append(c)

    lane = lax.broadcasted_iota(jnp.int32, (head_dim, 128), 1)
    for h in range(heads):
        state = jnp.dot(kt_ref[h], v_ref[h], preferred_element_type=jnp.float32)
        keepf = jnp.full((head_dim, 128), ret_ref[0, h], jnp.float32)
        high = keepf.astype(jnp.bfloat16).astype(jnp.float32)
        state = jnp.where(lane == head_dim + 1, high, state)
        state = jnp.where(lane == head_dim + 2, keepf - high, state)
        local[h * head_dim : (h + 1) * head_dim, :] = state
    for j in range(BLOCK):
        outbox[j] = local[j * rows : (j + 1) * rows, :].astype(jnp.bfloat16)
    pltpu.make_async_copy(outbox.at[spot], inbox.at[spot], lsem.at[1]).start()
    first = [
        send(outbox.at[m], inbox.at[spot], s1.at[m], r1.at[spot], device(layer * BLOCK + m)) for m in mates
    ]
    for c in first:
        c.start()
    across.wait()
    launch(1)

    pltpu.make_async_copy(outbox.at[spot], inbox.at[spot], lsem.at[1]).wait()
    for m in mates:
        send(outbox.at[m], inbox.at[m], s1.at[m], r1.at[m], device(layer * BLOCK + m)).wait_recv()
    wide = lax.broadcasted_iota(jnp.int32, (rows, 128), 1)

    def factor_of(x):
        return x[:, head_dim + 1 : head_dim + 2] + x[:, head_dim + 2 : head_dim + 3]

    running = jnp.zeros((rows, 128), jnp.float32)
    factor = jnp.ones((rows, 1), jnp.float32)
    factors = []
    for j in range(BLOCK):
        within[j] = running
        factors.append(factor)
        got = inbox[j].astype(jnp.float32)
        f = factor_of(got)
        running = f * running + got
        factor = factor * f
    full = jnp.broadcast_to(factor, (rows, 128))
    high = full.astype(jnp.bfloat16).astype(jnp.float32)
    total = jnp.where(wide == head_dim + 1, high, running)
    total = jnp.where(wide == head_dim + 2, full - high, total)
    tot_out[...] = total.astype(jnp.bfloat16)
    second = [
        send(tot_out, tot_in.at[layer], s2.at[o], r2.at[layer], device(o * BLOCK + spot)) for o in others
    ]
    for c in second:
        c.start()
    ring(1)
    for o in others:
        send(tot_out, tot_in.at[o], s2.at[o], r2.at[o], device(o * BLOCK + spot)).wait_recv()

    def earlier(i, carry):
        got = tot_in[i].astype(jnp.float32)
        return factor_of(got) * carry + got

    before = lax.fori_loop(0, layer, earlier, jnp.zeros((rows, 128), jnp.float32))
    for j in range(BLOCK):
        back_out[j] = (factors[j] * before + within[j]).astype(jnp.bfloat16)
    pltpu.make_async_copy(back_out.at[spot], back_in.at[spot], lsem.at[2]).start()
    third = [
        send(back_out.at[m], back_in.at[spot], s3.at[m], r3.at[spot], device(layer * BLOCK + m)) for m in mates
    ]
    for c in third:
        c.start()
    ring(1)
    pltpu.make_async_copy(back_out.at[spot], back_in.at[spot], lsem.at[2]).wait()
    for m in mates:
        send(back_out.at[m], back_in.at[m], s3.at[m], r3.at[m], device(layer * BLOCK + m)).wait_recv()
    for j in range(BLOCK):
        part = slice(j * rows, (j + 1) * rows)
        got = local[part, :]
        local[part, :] = factor_of(got) * back_in[j].astype(jnp.float32) + got

    ring(1)
    tokens = q_ref.shape[1]
    cut = heads * head_dim // groups
    depth = w_ref.shape[1]
    attend[...] = jnp.zeros_like(attend)
    squares = jnp.zeros((q_ref.shape[1], 1), jnp.float32)
    column = lax.broadcasted_iota(jnp.int32, (q_ref.shape[1], 128), 1)
    for h in range(heads):
        state = local[h * head_dim : (h + 1) * head_dim, :].astype(jnp.bfloat16)
        numer = jnp.dot(q_ref[h], state, preferred_element_type=jnp.float32)
        value = numer / (numer[:, head_dim : head_dim + 1] + 0.0001)
        value = jnp.where(column < head_dim, value, 0.0)
        squares = squares + jnp.sum(value * value, axis=1, keepdims=True)
        at, stop = h * head_dim, (h + 1) * head_dim
        while at < stop:
            block = at // cut
            end = min(stop, (block + 1) * cut)
            to = block * depth + at - block * cut
            attend[:, to : to + end - at] = value[:, at - h * head_dim : end - h * head_dim]
            at = end
    ring(1)
    scale = lax.rsqrt(squares / (heads * head_dim) + 1e-06)
    normed[...] = (attend[...] * scale).astype(jnp.bfloat16)
    keepn = pltpu.make_async_copy(normed, slot(core, span), lsem.at[3])
    keepn.start()
    peers = [(span + k) % members for k in range(1, members)]
    fourth = [
        send(normed, slot(core, span), sn.at[p], rn.at[span], (grp, p)) for p in peers
    ]
    for c in fourth:
        c.start()
    cross = [send(normed, slot(core, span), sc.at[span], rc.at[span], twin)]
    cross[0].start()
    ring(1)
    for p in peers:
        send(normed, slot(core, p), sn.at[p], rn.at[p], (grp, p)).wait_recv()
        c = send(slot(core, p), slot(core, p), sc.at[p], rc.at[p], twin)
        c.start()
        cross.append(c)
    keepn.wait()
    for p in [span] + peers:
        send(slot(1 - core, p), slot(1 - core, p), sc.at[p], rc.at[p], twin).wait_recv()

    middle = tokens // 2
    has = (chip > 0, chip < chips - 1)

    def edge(side, part):
        return nrm_ref.at[side * (2 * members + 1), pl.ds(pl.multiple_of(part * middle, middle), middle)]

    def edge_copy(side):
        source = nrm_ref.at[
            2 * members if side == 0 else 1, pl.ds(pl.multiple_of(core * middle, middle), middle)
        ]
        target = (2 * (chip + (1 if side == 0 else -1)) + core, span)
        return send(source, edge(side, core), se.at[side], re.at[side], target)

    def twin_copy(side, part):
        return send(edge(side, part), edge(side, part), st.at[side], rt.at[side], twin)

    for side in (0, 1):
        @pl.when(has[1 - side])
        def _(side=side):
            edge_copy(side).start()

    ring(1)

    for side in (0, 1):
        @pl.when(has[side])
        def _(side=side):
            edge_copy(side).wait_recv()
            twin_copy(side, core).start()

    ring(len(steps))
    for side in (0, 1):
        @pl.when(has[side])
        def _(side=side):
            twin_copy(side, 1 - core).wait_recv()
            twin_copy(side, core).wait_send()

        @pl.when(has[1 - side])
        def _(side=side):
            edge_copy(side).wait_send()

    keep.wait()
    for c in first + second + third + fourth + cross + started:
        c.wait_send()


def gather_and_attend(queries, key_rows, value_rows, retention, up_weight):
    groups = lax.axis_size("grp")
    members = lax.axis_size("span")
    tokens, dim = queries.shape
    heads = retention.shape[1]
    head_dim = dim // heads
    rows, _, width = up_weight.shape
    part = width // 2
    depth = -(-rows // 16) * 16
    kt = jnp.maximum(key_rows, 0).T.reshape(heads, head_dim, tokens)
    q = jnp.maximum(queries, 0).reshape(tokens, heads, head_dim).transpose(1, 0, 2)
    v = value_rows.reshape(tokens, heads, head_dim).transpose(1, 0, 2)
    rest = 128 - head_dim
    one = jnp.ones((heads, tokens, 1), v.dtype)
    v = jnp.concatenate([v, one, jnp.zeros((heads, tokens, rest - 1), v.dtype)], axis=2)
    w = up_weight.reshape(rows, 2, 2, part).transpose(2, 0, 1, 3).reshape(2, rows, width)
    w = jnp.pad(w, ((0, 0), (0, depth - rows), (0, 0)))
    chips = groups // 2
    share = dim // BLOCK
    layers = groups * members // BLOCK
    dma = pltpu.SemaphoreType.DMA
    vmem = pl.BlockSpec(memory_space=pltpu.VMEM)
    anywhere = pl.BlockSpec(memory_space=pl.ANY)
    bf = jnp.bfloat16
    slabs = pltpu.VMEM((BLOCK, share, 128), bf)
    weight, normed = pl.pallas_call(
        functools.partial(fused, groups, members, heads, head_dim),
        out_shape=(
            jax.ShapeDtypeStruct((chips, 2, depth, width), bf),
            jax.ShapeDtypeStruct((2 * members + 2, tokens, groups * depth), bf),
        ),
        in_specs=[vmem, vmem, vmem, pl.BlockSpec(memory_space=pltpu.SMEM), anywhere],
        out_specs=(anywhere, anywhere),
        scratch_shapes=[
            pltpu.VMEM((dim, 128), jnp.float32),
            slabs,
            slabs,
            pltpu.VMEM((share, 128), bf),
            pltpu.VMEM((layers, share, 128), bf),
            slabs,
            slabs,
            pltpu.VMEM((BLOCK, share, 128), jnp.float32),
            pltpu.VMEM((tokens, groups * depth), jnp.float32),
            pltpu.VMEM((tokens, groups * depth), bf),
            dma((BLOCK,)), dma((BLOCK,)),
            dma((layers,)), dma((layers,)),
            dma((BLOCK,)), dma((BLOCK,)),
            dma((2, chips // 2, 2)), dma((2, chips // 2, 2)),
            dma, dma,
            dma((members,)), dma((members,)),
            dma((members,)), dma((members,)),
            dma((2,)), dma((2,)),
            dma((2,)), dma((2,)),
            dma((4,)),
        ],
        compiler_params=pltpu.CompilerParams(
            collective_id=0, has_side_effects=True, vmem_limit_bytes=32 * 1024 * 1024
        ),
        name="gather_and_attend",
    )(kt, v, q, retention, w)
    weight = weight.reshape(groups * depth, width)
    return normed.reshape((2 * members + 2) * tokens, groups * depth), weight


def convolve(edges, xv, xg, tv, tg, cv, cg, out, pv, pg):
    frames = out.shape[0]
    for x, pad in ((xv, pv), (xg, pg)):
        pad[:, 0:1] = jnp.zeros_like(pad[:, 0:1])
        pad[:, FH + 1 :] = jnp.zeros_like(pad[:, FH + 1 :])
        pad[1 : frames + 1, 1 : FH + 1] = x[1 : frames + 1].astype(jnp.float32)
        for side, k in ((0, 0), (1, frames + 1)):
            pad[k, 1 : FH + 1] = jnp.where(edges[0, side] > 0, x[k].astype(jnp.float32), 0.0)
    tile = out.shape[-1]
    column = lax.broadcasted_iota(jnp.int32, (FH, FW, tile), 1)

    def mix(pad, taps, bias, k):
        sums = [None, None, None]
        for a in range(3):
            for b in range(3):
                slab = pad[k + a, b : b + FH]
                for e in range(3):
                    term = slab * taps[a * 9 + b * 3 + e : a * 9 + b * 3 + e + 1, :].reshape(1, 1, tile)
                    sums[e] = term if sums[e] is None else sums[e] + term
        lower = jnp.where(column > 0, pltpu.roll(sums[0], 1, 1), 0.0)
        upper = jnp.where(column < FW - 1, pltpu.roll(sums[2], FW - 1, 1), 0.0)
        return bias[...].reshape(1, 1, tile) + sums[1] + lower + upper

    @pl.loop(0, frames)
    def _(k):
        value = mix(pv, tv, cv, k)
        gate = mix(pg, tg, cg, k)
        out[k] = (value * (gate / (1.0 + jnp.exp(-gate)))).astype(out.dtype)


def conv_gate(edges, grid, taps, bias):
    frames = grid.shape[0] - 2
    part = grid.shape[-1] // 2
    tile = 256 if part % 256 == 0 else 128 if part % 128 == 0 else part
    operands, specs = [edges], [pl.BlockSpec(memory_space=pltpu.SMEM)]
    for x in (grid, taps, bias):
        lead = (0,) * (x.ndim - 1)
        for j in (0, 1):
            shift = j * part // tile if tile < part else 0
            operands.append(x if tile < part else x[..., j * part : (j + 1) * part])
            specs.append(pl.BlockSpec(x.shape[:-1] + (tile,), lambda i, lead=lead, shift=shift: lead + (i + shift,)))
    return pl.pallas_call(
        convolve,
        grid=(part // tile,),
        out_shape=jax.ShapeDtypeStruct((frames, FH, FW, part), jnp.bfloat16),
        in_specs=specs,
        out_specs=pl.BlockSpec((frames, FH, FW, tile), lambda i: (0, 0, 0, i)),
        scratch_shapes=[pltpu.VMEM((frames + 2, FH + 2, FW, tile), jnp.float32)] * 2,
        compiler_params=pltpu.CompilerParams(vmem_limit_bytes=40 * 1024 * 1024),
        name="conv_gate",
    )(*operands)


def shards(queries, key_rows, value_rows, retention, up_weight, conv_weight, conv_bias):
    normed, flat_weight = gather_and_attend(queries, key_rows, value_rows, retention, up_weight)
    groups = lax.axis_size("grp")
    core = lax.axis_index("grp") % 2
    up_vals = jnp.dot(normed, flat_weight, preferred_element_type=jnp.float32)
    up_vals = up_vals.astype(jnp.bfloat16)
    part = flat_weight.shape[1] // 2
    frames = up_vals.shape[0] // (FH * FW) - 2
    grid = up_vals.reshape(frames + 2, FH, FW, 2 * part)
    group = lax.axis_index("grp")
    edges = jnp.stack([group >= 2, group < groups - 2]).astype(jnp.int32).reshape(1, 2)
    taps = lax.dynamic_slice_in_dim(conv_weight, core * part, part, axis=4)
    convolution_kernel = taps.reshape(27, 2 * part).astype(jnp.float32)
    bias = lax.dynamic_slice_in_dim(conv_bias, core * part, part, axis=1)
    hidden = conv_gate(edges, grid, convolution_kernel, bias.reshape(1, 2 * part))
    hidden = hidden.reshape(2, frames * FH * FW // 2, part)
    mine = lax.dynamic_index_in_dim(hidden, core, 0, False)
    theirs = swap(lax.dynamic_index_in_dim(hidden, 1 - core, 0, False), groups)
    first = jnp.where(core == 0, mine, theirs)
    second = jnp.where(core == 0, theirs, mine)
    return jnp.concatenate([first, second], axis=1)


def solution(mesh):
    in_specs = (
        P(("grp", "span"), None),
        P(("grp", "span"), None),
        P(("grp", "span"), None),
        P(("grp", "span"), None),
        P("grp", None, "span"),
        P(None, None, None, None, "span"),
        P(None, "span"),
    )
    out_specs = P("grp", "span")
    return jax.shard_map(shards, mesh=mesh, in_specs=in_specs, out_specs=out_specs, check_vma=False)
```
